128 devices in a mesh: feat: 32 (over z, x, core), conf: 4 (over y).
Axes of the slice: x: 4, y: 4, z: 4, core: 2. Of those that a mesh axis runs over, the one named last changes fastest.
Arguments:
- matrix: float32 [32768, 20480], P('conf', 'feat'), may hold values from -3 to 3
- targets: float32 [32, 32768], P(None, 'conf'), may hold values from -40 to 40
Outputs:
- solution: float32 [32, 20480], P(None, 'feat')
- residual: float32 [32, 32768], P(None, 'conf')
The draws below stay inside these ranges and needn't reach their ends.
All inputs are finite; a program needn't handle non-finite values.
Results may differ from the reference program's by a relative error of at most 0.00016.
Values sent between devices are 32-bit elements; how exact they have to be, the bound alone decides.
No kernel may reach another device: no remote copies, remote signals or barrier semaphores. Data moves between devices by JAX's collectives and lax.ppermute only.
A program may use at most 128 MiB of HBM per device.

```python
import math
import jax
import jax.numpy as jnp
from jax import lax

FEATURES = 20480
FITS = 32
ITERS = 2
ROWS = 32768


def draw_matrix(key, part):
    key = jax.random.fold_in(key, 11)
    row_key = jax.random.fold_in(key, 1)
    col_key = jax.random.fold_in(key, 2)
    entry_key = jax.random.fold_in(key, 3)
    row_rise = jnp.exp(math.log(3.0) * jnp.arange(ROWS, dtype=jnp.float32) / ROWS)[:, None]
    col_rise = jnp.exp(math.log(3.0) * jnp.arange(FEATURES, dtype=jnp.float32) / FEATURES)[None, :]
    row_scale = jnp.exp(math.log(10.0) * jax.random.uniform(row_key, (ROWS, 1), jnp.float32)) * row_rise
    col_scale = jnp.exp(math.log(10.0) * jax.random.uniform(col_key, (1, FEATURES), jnp.float32)) * col_rise
    entries = jnp.clip(jax.random.normal(entry_key, (ROWS, FEATURES), jnp.float32), -5.0, 5.0)
    return jnp.clip(entries * row_scale * col_scale / (15.0 * math.sqrt(FEATURES)), -3.0, 3.0)


def draw_targets(key, part):
    key = jax.random.fold_in(key, 23)
    scale_key = jax.random.fold_in(key, 1)
    entry_key = jax.random.fold_in(key, 2)
    rise = jnp.exp(math.log(3.0) * jnp.arange(ROWS, dtype=jnp.float32) / ROWS)[None, :]
    scales = jnp.exp(math.log(10.0) * jax.random.uniform(scale_key, (1, ROWS), jnp.float32)) * rise
    entries = jnp.clip(jax.random.normal(entry_key, (FITS, ROWS), jnp.float32), -5.0, 5.0)
    return entries * scales / 4.0


def setup_inputs(seed: int = 0) -> dict:
    splits = jax.random.split(jax.random.key(seed), 3)
    return {
        "matrix": draw_matrix(jax.random.fold_in(splits[2], 71), 0),
        "targets": draw_targets(jax.random.fold_in(splits[2], 71), 0),
    }


def apply_rows(vectors, matrix):
    return lax.dot_general(vectors, matrix, (((1,), (1,)), ((), ())), precision=lax.Precision.HIGHEST, preferred_element_type=jnp.float32)


def apply_cols(vectors, matrix):
    return jnp.dot(vectors, matrix, precision=lax.Precision.HIGHEST, preferred_element_type=jnp.float32)


def reference(matrix, targets):
    residual = targets
    gradient = apply_cols(residual, matrix)
    direction = gradient
    grad_norm = jnp.sum(gradient * gradient, axis=1)
    solution = jnp.zeros((targets.shape[0], matrix.shape[1]), jnp.float32)
    for sweep in range(ITERS):
        image = apply_rows(direction, matrix)
        curve_sum = jnp.sum(image * image, axis=1)
        step_size = grad_norm / curve_sum
        solution = solution + step_size[:, None] * direction
        residual = residual - step_size[:, None] * image
        gradient = apply_cols(residual, matrix)
        grad_next = jnp.sum(gradient * gradient, axis=1)
        direction = gradient + (grad_next / grad_norm)[:, None] * direction
        grad_norm = grad_next
    return solution, residual
```

```python
import functools

import jax
import jax.numpy as jnp
from jax import lax
from jax.experimental import pallas as pl
from jax.experimental.pallas import tpu as pltpu
from jax.sharding import PartitionSpec as P

BF, F32 = jnp.bfloat16, jnp.float32
MEMBERS = 32
PIECES = 4
PAD = 128
VMEM = pl.BlockSpec(memory_space=pltpu.VMEM)
SMEM = pl.BlockSpec(memory_space=pltpu.SMEM)
ANY = pl.BlockSpec(memory_space=pl.ANY)


def params(mib):
    return pltpu.CompilerParams(vmem_limit_bytes=mib << 20)


def pin(x):
    return pltpu.with_memory_space_constraint(x, pltpu.VMEM)


def split(x, parts):
    out = []
    for _ in range(parts - 1):
        high = x.astype(BF)
        out.append(high)
        x = x - high.astype(F32)
    return out + [x.astype(BF)]


def fold(product, parts):
    n = product.shape[1] // 2
    rows = sum(product[MEMBERS * j : MEMBERS * (j + 1)] for j in range(parts))
    return rows[:, :n] + rows[:, n:]


def first_kernel(
    blocks, depth, parts, meta, r_hbm, m_hbm, pair_ref, g_ref, r_buf, m_buf, acc_ref, r_sem, m_sem
):
    rows, n = m_hbm.shape
    block = rows // blocks

    def at(i):
        return pl.ds(pl.multiple_of(i * block, block), block)

    def copies(i):
        slot = lax.rem(i, depth)
        return [
            pltpu.make_async_copy(m_hbm.at[at(i)], m_buf.at[slot], m_sem.at[slot]),
            pltpu.make_async_copy(r_hbm.at[:, at(i)], r_buf.at[slot], r_sem.at[slot]),
        ]

    def begin(i):
        for copy in copies(i):
            copy.start()

    def place(i):
        for copy in copies(i):
            copy.wait()
        pair_ref[at(i), :] = jnp.concatenate(split(m_buf[lax.rem(i, depth)], 2), axis=1)

    def add(i):
        vectors = jnp.concatenate(split(r_buf[lax.rem(i, depth)], parts), axis=0)
        acc_ref[...] += jnp.dot(vectors, pair_ref[at(i), :], preferred_element_type=F32)

    for i in range(depth):
        begin(i)
    acc_ref[...] = jnp.zeros_like(acc_ref)
    place(0)

    def step(i, carry):
        add(i - 1)
        place(i)

        @pl.when(i + depth - 1 < blocks)
        def _():
            begin(i + depth - 1)

        return carry

    lax.fori_loop(1, blocks, step, 0)
    add(blocks - 1)
    g_ref[...] = fold(acc_ref[...], parts)


def first(meta, residual, matrix, blocks=16, depth=4, parts=3):
    rows, n = matrix.shape
    block = rows // blocks
    return pl.pallas_call(
        functools.partial(first_kernel, blocks, depth, parts),
        in_specs=[SMEM, ANY, ANY],
        out_specs=[VMEM, VMEM],
        out_shape=[pltpu.VMEM((rows, 2 * n), BF), pltpu.VMEM((MEMBERS, n), F32)],
        scratch_shapes=[
            pltpu.VMEM((depth, MEMBERS, block), F32),
            pltpu.VMEM((depth, block, n), F32),
            pltpu.VMEM((MEMBERS * parts, 2 * n), F32),
            pltpu.SemaphoreType.DMA((depth,)),
            pltpu.SemaphoreType.DMA((depth,)),
        ],
        compiler_params=params(16),
    )(meta, residual, matrix)


def rows_body(half, start, d, pair_ref, out_ref, w_ref):
    n = d.shape[1]
    piece = out_ref.shape[2] - PAD
    t = jnp.concatenate([x.astype(F32) for x in split(d, 2)], axis=0).T.astype(BF)
    w_ref[:n, :] = t
    w_ref[n:, :] = t
    chunk = 512
    norm = jnp.broadcast_to(jnp.sum(d * d, axis=1, keepdims=True), (MEMBERS, PAD))
    for q in range(PIECES):
        slot = lax.rem(q - start + PIECES, PIECES)
        for r in range(0, piece, chunk):
            at = pl.multiple_of((half * PIECES + q) * piece + r, chunk)
            o = jnp.dot(
                pair_ref[pl.ds(at, chunk), :], w_ref[...], preferred_element_type=F32
            ).T
            out_ref[slot, :, r : r + chunk] = o[:MEMBERS] + o[MEMBERS:]
        out_ref[slot, :, piece:] = norm


def rows_kernel(place, meta, d_ref, pair_ref, out_ref, w_ref):
    rows_body(meta[2 * place], meta[2 * place + 1], d_ref[...], pair_ref, out_ref, w_ref)


def rows_first_kernel(place, meta, a, b, c, d, pair_ref, out_ref, g_ref, w_ref):
    g = (a[...] + c[...]) + (b[...] + d[...])
    g_ref[...] = g
    rows_body(meta[2 * place], meta[2 * place + 1], g, pair_ref, out_ref, w_ref)


def rows_second_kernel(
    place, meta, a, b, c, d, g0_ref, gamma_ref, pair_ref, out_ref, g_ref, alpha_ref, w_ref
):
    w = (a[...] + c[...]) + (b[...] + d[...])
    n = g0_ref.shape[1]
    alpha = gamma_ref[...] / w[:, n:]
    alpha_ref[...] = alpha
    g = g0_ref[...] - alpha[:, :1] * w[:, :n]
    g_ref[...] = g
    rows_body(meta[2 * place], meta[2 * place + 1], g, pair_ref, out_ref, w_ref)


def by_rows(kernel, place, meta, operands, pair, more):
    rows, n2 = pair.shape
    piece = rows // (2 * PIECES)
    return pl.pallas_call(
        functools.partial(kernel, place),
        in_specs=[SMEM] + [VMEM] * (len(operands) + 1),
        out_specs=[VMEM] * (1 + len(more)),
        out_shape=[pltpu.VMEM((PIECES, MEMBERS, piece + PAD), F32)]
        + [pltpu.VMEM(s, F32) for s in more],
        scratch_shapes=[pltpu.VMEM((n2, 2 * MEMBERS), BF)],
        compiler_params=params(16),
    )(meta, *map(pin, operands), pin(pair))


def cols_body(half, start, pieces, pair_ref, parts):
    piece = pieces[0].shape[1]
    acc = jnp.zeros((MEMBERS * parts, pair_ref.shape[1]), F32)
    norm = jnp.zeros((MEMBERS, 1), F32)
    for i, p in enumerate(pieces):
        q = lax.rem(start - i + PIECES, PIECES)
        at = pl.multiple_of((half * PIECES + q) * piece, piece)
        vectors = jnp.concatenate(split(p, parts), axis=0)
        acc += jnp.dot(vectors, pair_ref[pl.ds(at, piece), :], preferred_element_type=F32)
        norm += jnp.sum(p * p, axis=1, keepdims=True)
    return fold(acc, parts), norm


def cols_own_kernel(parts, meta, a, b, c, d, pair_ref, w_ref):
    w, norm = cols_body(meta[0], meta[1], [a[...], b[...], c[...], d[...]], pair_ref, parts)
    n = w.shape[1]
    w_ref[:, :n] = w
    w_ref[:, n:] = jnp.broadcast_to(norm, (MEMBERS, PAD))


def cols_other_kernel(parts, meta, p_ref, before_ref, pair_ref, w_ref):
    w, norm = cols_body(
        meta[2], meta[3], [p_ref[i] for i in range(PIECES)], pair_ref, parts
    )
    n = w.shape[1]
    w_ref[:, :n] = before_ref[:, :n] + w
    w_ref[:, n:] = before_ref[:, n:] + norm


def by_cols(kernel, meta, operands, pair, parts=3):
    n = pair.shape[1] // 2
    return pl.pallas_call(
        functools.partial(kernel, parts),
        in_specs=[SMEM] + [VMEM] * (len(operands) + 1),
        out_specs=VMEM,
        out_shape=pltpu.VMEM((MEMBERS, n + PAD), F32),
        compiler_params=params(16),
    )(meta, *map(pin, operands), pin(pair))


def ring(stage):
    def moved(f, k):
        z, x, core = f // 8, f // 2 % 4, f % 2
        if core == stage:
            z = (z + k) % 4
        else:
            x = (x + k) % 4
        return z * 8 + x * 2 + core

    return [[(f, moved(f, k)) for f in range(32)] for k in (1, 2, 3)]


CORE = [(f, f ^ 1) for f in range(32)]
CONF = [[(c, (c + k) % 4) for c in range(4)] for k in (1, 2, 3)]


def three(xs, axis, perms):
    return [lax.ppermute(x, axis, perm) for x, perm in zip(xs, perms)]


def total(own, others):
    return (own + others[1]) + (others[0] + others[2])


def reduce_pieces(keep, send):
    got = lax.ppermute(send, "feat", CORE)
    mine = [keep[i] + got[i] for i in range(PIECES)]
    piece = total(mine[0], three(mine[1:], "feat", ring(0)))
    return total(piece, three([piece] * 3, "feat", ring(1)))


def gather_pieces(piece):
    own = [piece] + three([piece] * 3, "feat", ring(0))
    return own, lax.ppermute(jnp.stack(own), "feat", CORE)


def finish_kernel(*refs):
    meta, r0_ref, coef = refs[0], refs[1], refs[2]
    p_own, p_other, i_own, i_other = refs[3:7], refs[7], refs[8:12], refs[12]
    g0_ref, g1_ref, sol_ref, res_ref = refs[13:]
    a0, a1, b0 = coef[0, :, :1], coef[1, :, :1], coef[2, :, :1]
    g0 = g0_ref[...]
    sol_ref[...] = a0 * g0 + a1 * (g1_ref[...] + b0 * g0)
    piece = p_own[0].shape[1]
    for half in range(2):
        for i in range(PIECES):
            q = lax.rem(meta[2 * half + 1] - i + PIECES, PIECES)
            at = pl.multiple_of((meta[2 * half] * PIECES + q) * piece, piece)
            p = p_other[i] if half else p_own[i][...]
            image = i_other[i] if half else i_own[i][...]
            res_ref[:, pl.ds(at, piece)] = (
                r0_ref[:, pl.ds(at, piece)] - a0 * p - a1 * image
            )


def body(matrix, targets):
    f = lax.axis_index("feat")
    z, x, core = f // 8, f // 2 % 4, f % 2
    mine = jnp.where(core == 0, z, x)
    other = jnp.where(core == 0, x, z)
    meta = jnp.stack([core, mine, 1 - core, other]).astype(jnp.int32)
    rows, n = matrix.shape
    piece = rows // (2 * PIECES)

    pair, part = first(meta, targets, matrix)
    parts = [part] + three([part] * 3, "conf", CONF)

    send, g0 = by_rows(rows_first_kernel, 1, meta, parts, pair, [(MEMBERS, n)])
    (keep,) = by_rows(rows_kernel, 0, meta, [g0], pair, [])
    p = reduce_pieces(keep, send)
    gamma0 = p[:, piece:]
    p = p[:, :piece]
    p_own, p_other = gather_pieces(p)

    w = by_cols(cols_own_kernel, meta, p_own, pair)
    w = by_cols(cols_other_kernel, meta, [p_other, w], pair)
    parts = [w] + three([w] * 3, "conf", CONF)

    send, g1, alpha0 = by_rows(
        rows_second_kernel,
        1,
        meta,
        parts + [g0, gamma0],
        pair,
        [(MEMBERS, n), (MEMBERS, PAD)],
    )
    (keep,) = by_rows(rows_kernel, 0, meta, [g1], pair, [])
    image = reduce_pieces(keep, send)
    gamma1 = image[:, piece:]
    beta = gamma1 / gamma0
    image = image[:, :piece] + beta[:, :1] * p
    i_own, i_other = gather_pieces(image)

    curve = sum(jnp.sum(v * v, axis=1, keepdims=True) for v in i_own)
    curve = curve + jnp.sum(jnp.sum(i_other * i_other, axis=0), axis=1, keepdims=True)
    curve = jnp.broadcast_to(curve, (MEMBERS, PAD))
    curve = total(curve, three([curve] * 3, "conf", CONF))
    alpha1 = gamma1 / curve
    coef = jnp.stack([alpha0, alpha1, beta])

    return pl.pallas_call(
        finish_kernel,
        in_specs=[SMEM] + [VMEM] * 14,
        out_specs=[VMEM, VMEM],
        out_shape=[
            jax.ShapeDtypeStruct((MEMBERS, n), F32),
            jax.ShapeDtypeStruct((MEMBERS, rows), F32),
        ],
        compiler_params=params(16),
    )(meta, targets, coef, *p_own, p_other, *i_own, i_other, g0, g1)


def solution(mesh):
    placed = (P("conf", "feat"), P(None, "conf"))
    return jax.shard_map(
        body,
        mesh=mesh,
        in_specs=placed,
        out_specs=(P(None, "feat"), P(None, "conf")),
        check_vma=False,
    )
```

```python
import functools

import jax
import jax.numpy as jnp
from jax import lax
from jax.experimental import pallas as pl
from jax.experimental.pallas import tpu as pltpu
from jax.sharding import PartitionSpec as P

BF, F32 = jnp.bfloat16, jnp.float32
MEMBERS = 32
PIECES = 4
PAD = 128
VMEM = pl.BlockSpec(memory_space=pltpu.VMEM)
ANY = pl.BlockSpec(memory_space=pl.ANY)


def params(mib):
    return pltpu.CompilerParams(vmem_limit_bytes=mib << 20)


def pin(x):
    return pltpu.with_memory_space_constraint(x, pltpu.VMEM)


def far(x):
    return pltpu.with_memory_space_constraint(x, pltpu.HBM)


def place(other):
    f = lax.axis_index("feat")
    z, x, core = f // 8, f // 2 % 4, f % 2
    return core ^ other, jnp.where((core ^ other) == 0, z, x)


def split(x, parts):
    out = []
    for _ in range(parts - 1):
        high = x.astype(BF)
        out.append(high)
        x = x - high.astype(F32)
    return out + [x.astype(BF)]


def fold(product, parts):
    n = product.shape[1] // 2
    rows = sum(product[MEMBERS * j : MEMBERS * (j + 1)] for j in range(parts))
    return rows[:, :n] + rows[:, n:]


def first_kernel(
    blocks, depth, chunk, parts, r_hbm, m_hbm, pair_ref, g_ref, r_ref, m_buf, acc_ref, r_sem, m_sem
):
    rows, n = m_hbm.shape
    block = rows // blocks

    def copy(i):
        slot = lax.rem(i, depth)
        at = pl.ds(pl.multiple_of(i * block, block), block)
        return pltpu.make_async_copy(m_hbm.at[at], m_buf.at[slot], m_sem.at[slot])

    vectors = pltpu.make_async_copy(r_hbm, r_ref, r_sem)
    copy(0).start()
    vectors.start()
    for i in range(1, depth):
        copy(i).start()
    acc_ref[...] = jnp.zeros_like(acc_ref)
    vectors.wait()

    def step(i, carry):
        copy(i).wait()
        slot = lax.rem(i, depth)
        for k in range(0, block, chunk):
            at = pl.ds(pl.multiple_of(i * block + k, chunk), chunk)
            pair = jnp.concatenate(split(m_buf[slot, k : k + chunk, :], 2), axis=1)
            pair_ref[at, :] = pair
            r = jnp.concatenate(split(r_ref[:, at], parts), axis=0)
            acc_ref[...] += jnp.dot(r, pair, preferred_element_type=F32)

        @pl.when(i + depth < blocks)
        def _():
            copy(i + depth).start()

        return carry

    lax.fori_loop(0, blocks, step, 0)
    g_ref[...] = fold(acc_ref[...], parts)


def first(residual, matrix, blocks=8, depth=3, chunk=512, parts=3):
    rows, n = matrix.shape
    return pl.pallas_call(
        functools.partial(first_kernel, blocks, depth, chunk, parts),
        in_specs=[ANY, ANY],
        out_specs=[VMEM, VMEM],
        out_shape=[pltpu.VMEM((rows, 2 * n), BF), pltpu.VMEM((MEMBERS, n), F32)],
        scratch_shapes=[
            pltpu.VMEM(residual.shape, F32),
            pltpu.VMEM((depth, rows // blocks, n), F32),
            pltpu.VMEM((MEMBERS * parts, 2 * n), F32),
            pltpu.SemaphoreType.DMA,
            pltpu.SemaphoreType.DMA((depth,)),
        ],
        compiler_params=params(20),
    )(far(residual), far(matrix))


def rows_body(half, start, d, pair_ref, out_ref, w_ref):
    n = d.shape[1]
    piece = out_ref.shape[2] - PAD
    t = jnp.concatenate([x.astype(F32) for x in split(d, 2)], axis=0).T.astype(BF)
    w_ref[:n, :] = t
    w_ref[n:, :] = t
    chunk = 512
    norm = jnp.broadcast_to(jnp.sum(d * d, axis=1, keepdims=True), (MEMBERS, PAD))
    for q in range(PIECES):
        slot = lax.rem(q - start + PIECES, PIECES)
        for r in range(0, piece, chunk):
            at = pl.multiple_of((half * PIECES + q) * piece + r, chunk)
            o = jnp.dot(
                pair_ref[pl.ds(at, chunk), :], w_ref[...], preferred_element_type=F32
            ).T
            out_ref[slot, :, r : r + chunk] = o[:MEMBERS] + o[MEMBERS:]
        out_ref[slot, :, piece:] = norm


def rows_kernel(other, d_ref, pair_ref, out_ref, w_ref):
    rows_body(*place(other), d_ref[...], pair_ref, out_ref, w_ref)


def rows_first_kernel(other, a, b, c, d, pair_ref, out_ref, g_ref, w_ref):
    g = (a[...] + d[...]) + (b[...] + c[...])
    g_ref[...] = g
    rows_body(*place(other), g, pair_ref, out_ref, w_ref)


def rows_second_kernel(
    other, a, b, c, d, g0_ref, gamma_ref, pair_ref, out_ref, g_ref, alpha_ref, w_ref
):
    w = (a[...] + d[...]) + (b[...] + c[...])
    n = g0_ref.shape[1]
    alpha = gamma_ref[...] / w[:, n:]
    alpha_ref[...] = alpha
    g = g0_ref[...] - alpha[:, :1] * w[:, :n]
    g_ref[...] = g
    rows_body(*place(other), g, pair_ref, out_ref, w_ref)


def by_rows(kernel, other, operands, pair, more):
    rows, n2 = pair.shape
    piece = rows // (2 * PIECES)
    return pl.pallas_call(
        functools.partial(kernel, other),
        in_specs=[VMEM] * (len(operands) + 1),
        out_specs=[VMEM] * (1 + len(more)),
        out_shape=[pltpu.VMEM((PIECES, MEMBERS, piece + PAD), F32)]
        + [pltpu.VMEM(s, F32) for s in more],
        scratch_shapes=[pltpu.VMEM((n2, 2 * MEMBERS), BF)],
        compiler_params=params(16),
    )(*map(pin, operands), pin(pair))


def cols_body(half, start, pieces, pair_ref, parts):
    piece = pieces[0].shape[1]
    acc = jnp.zeros((MEMBERS * parts, pair_ref.shape[1]), F32)
    norm = jnp.zeros((MEMBERS, 1), F32)
    for i, p in enumerate(pieces):
        q = lax.rem(start - ORDER[i] + PIECES, PIECES)
        at = pl.multiple_of((half * PIECES + q) * piece, piece)
        vectors = jnp.concatenate(split(p, parts), axis=0)
        acc += jnp.dot(vectors, pair_ref[pl.ds(at, piece), :], preferred_element_type=F32)
        norm += jnp.sum(p * p, axis=1, keepdims=True)
    return fold(acc, parts), norm


def cols_own_kernel(parts, a, b, c, d, pair_ref, w_ref):
    w, norm = cols_body(*place(0), [a[...], b[...], c[...], d[...]], pair_ref, parts)
    n = w.shape[1]
    w_ref[:, :n] = w
    w_ref[:, n:] = jnp.broadcast_to(norm, (MEMBERS, PAD))


def cols_other_kernel(parts, p_ref, before_ref, pair_ref, w_ref):
    w, norm = cols_body(*place(1), [p_ref[i] for i in range(PIECES)], pair_ref, parts)
    n = w.shape[1]
    w_ref[:, :n] = before_ref[:, :n] + w
    w_ref[:, n:] = before_ref[:, n:] + norm


def by_cols(kernel, operands, pair, parts=3):
    n = pair.shape[1] // 2
    return pl.pallas_call(
        functools.partial(kernel, parts),
        in_specs=[VMEM] * (len(operands) + 1),
        out_specs=VMEM,
        out_shape=pltpu.VMEM((MEMBERS, n + PAD), F32),
        compiler_params=params(16),
    )(*map(pin, operands), pin(pair))


def ring(stage):
    def moved(f, k):
        z, x, core = f // 8, f // 2 % 4, f % 2
        if core == stage:
            z = (z + k) % 4
        else:
            x = (x + k) % 4
        return z * 8 + x * 2 + core

    return [[(f, moved(f, k)) for f in range(32)] for k in (1, 2, 3)]


CORE = [(f, f ^ 1) for f in range(32)]
CONF = [[(c, (c + k) % 4) for c in range(4)] for k in (1, 2, 3)]


def three(xs, axis, perms):
    return [lax.ppermute(x, axis, perm) for x, perm in zip(xs, perms)]


ORDER = (0, 1, 3, 2)


def opposite_last(x):
    return [x[k] for k in ORDER]


def total(own, others):
    return (others[0] + others[2]) + (own + others[1])


def reduce_pieces(keep, send):
    got = lax.ppermute(send, "feat", CORE)
    mine = [keep[i] + got[i] for i in range(PIECES)]
    a, b, c, d = [mine[0]] + three(mine[1:], "feat", ring(0))
    piece = (b + d) + (a + c)
    return total(piece, three([piece] * 3, "feat", ring(1)))


def gather_pieces(piece):
    own = opposite_last([piece] + three([piece] * 3, "feat", ring(0)))
    return own, jnp.stack(own)


def finish_kernel(*refs):
    r0_ref, alpha0_ref, gamma0_ref, gamma1_ref, own_ref, other_ref = refs[:6]
    p_own, p_other, i_own, i_other = refs[6:10], refs[10], refs[11:15], refs[15]
    g0_ref, g1_ref, sol_ref, res_ref = refs[16:]
    gamma1 = gamma1_ref[:, :1]
    a0 = alpha0_ref[:, :1]
    a1 = gamma1 / (own_ref[:, :1] + other_ref[:, :1])
    b0 = gamma1 / gamma0_ref[:, :1]
    g0 = g0_ref[...]
    sol_ref[...] = a0 * g0 + a1 * (g1_ref[...] + b0 * g0)
    piece = p_own[0].shape[1]
    for far_half in range(2):
        half, start = place(far_half)
        for i in range(PIECES):
            q = lax.rem(start - ORDER[i] + PIECES, PIECES)
            at = pl.ds(pl.multiple_of((half * PIECES + q) * piece, piece), piece)
            p = p_other[i] if far_half else p_own[i][...]
            image = i_other[i] if far_half else i_own[i][...]
            res_ref[:, at] = r0_ref[:, at] - a0 * p - a1 * image


def body(matrix, targets):
    rows, n = matrix.shape
    piece = rows // (2 * PIECES)

    pair, part = first(targets, matrix)
    parts = opposite_last([part] + three([part] * 3, "conf", CONF))

    send, g0 = by_rows(rows_first_kernel, 1, parts, pair, [(MEMBERS, n)])
    (keep,) = by_rows(rows_kernel, 0, [g0], pair, [])
    p = reduce_pieces(keep, send)
    gamma0 = p[:, piece:]
    p = p[:, :piece]
    p_own, stacked = gather_pieces(p)
    p_other = lax.ppermute(stacked, "feat", CORE)

    w = by_cols(cols_own_kernel, p_own, pair)
    w = by_cols(cols_other_kernel, [p_other, w], pair)
    parts = opposite_last([w] + three([w] * 3, "conf", CONF))

    send, g1, alpha0 = by_rows(
        rows_second_kernel, 1, parts + [g0, gamma0], pair, [(MEMBERS, n), (MEMBERS, PAD)]
    )
    (keep,) = by_rows(rows_kernel, 0, [g1], pair, [])
    image = reduce_pieces(keep, send)
    gamma1 = image[:, piece:]
    beta = gamma1 / gamma0
    image = image[:, :piece] + beta[:, :1] * p
    i_own, stacked = gather_pieces(image)
    i_other = lax.ppermute(stacked, "feat", CORE)

    curve = sum(jnp.sum(v * v, axis=1, keepdims=True) for v in i_own)
    curve = jnp.broadcast_to(curve, (MEMBERS, PAD))
    curve = total(curve, three([curve] * 3, "conf", CONF))
    curve_other = lax.ppermute(curve, "feat", CORE)

    return pl.pallas_call(
        finish_kernel,
        in_specs=[VMEM] * 18,
        out_specs=[VMEM, VMEM],
        out_shape=[
            jax.ShapeDtypeStruct((MEMBERS, n), F32),
            jax.ShapeDtypeStruct((MEMBERS, rows), F32),
        ],
        compiler_params=params(16),
    )(
        targets,
        alpha0,
        gamma0,
        gamma1,
        curve,
        curve_other,
        *p_own,
        p_other,
        *i_own,
        i_other,
        g0,
        g1,
    )


def solution(mesh):
    placed = (P("conf", "feat"), P(None, "conf"))
    return jax.shard_map(
        body,
        mesh=mesh,
        in_specs=placed,
        out_specs=(P(None, "feat"), P(None, "conf")),
        check_vma=False,
    )
```

```python
import functools

import jax
import jax.numpy as jnp
from jax import lax
from jax.experimental import pallas as pl
from jax.experimental.pallas import tpu as pltpu
from jax.sharding import PartitionSpec as P

BF, F32 = jnp.bfloat16, jnp.float32
MEMBERS = 32
PIECES = 4
LANES = 128
TAIL = 8
VMEM = pl.BlockSpec(memory_space=pltpu.VMEM)
ANY = pl.BlockSpec(memory_space=pl.ANY)


def params(mib):
    return pltpu.CompilerParams(vmem_limit_bytes=mib << 20)


def pin(x):
    return pltpu.with_memory_space_constraint(x, pltpu.VMEM)


def far(x):
    return pltpu.with_memory_space_constraint(x, pltpu.HBM)


def place(other):
    f = lax.axis_index("feat")
    z, x, core = f // 8, f // 2 % 4, f % 2
    return core ^ other, jnp.where((core ^ other) == 0, z, x)


def split(x, parts):
    out = []
    for _ in range(parts - 1):
        high = x.astype(BF)
        out.append(high)
        x = x - high.astype(F32)
    return out + [x.astype(BF)]


def fold(product, parts):
    n = product.shape[1] // 2
    rows = sum(product[MEMBERS * j : MEMBERS * (j + 1)] for j in range(parts))
    return rows[:, :n] + rows[:, n:]


def strips(packed_ref, width):
    at = range(0, width // LANES * MEMBERS, MEMBERS)
    return jnp.concatenate([packed_ref[i : i + MEMBERS, :] for i in at], axis=1)


def put(packed_ref, values, first=0):
    for j in range(values.shape[1] // LANES):
        at = (first + j) * MEMBERS
        packed_ref[at : at + MEMBERS, :] = values[:, j * LANES : (j + 1) * LANES]


def put_sums(packed_ref, column):
    groups = MEMBERS // TAIL
    blocks = [column[TAIL * k : TAIL * (k + 1)] for k in range(groups)]
    blocks = [jnp.broadcast_to(b, (TAIL, LANES // groups)) for b in blocks]
    packed_ref[packed_ref.shape[0] - TAIL :, :] = jnp.concatenate(blocks, axis=1)


def sums_of(packed):
    groups = MEMBERS // TAIL
    block, width = packed[packed.shape[0] - TAIL :, :], LANES // groups
    return jnp.concatenate(
        [block[:, k * width : k * width + 1] for k in range(groups)], axis=0
    )


def wide(column):
    return jnp.broadcast_to(column, (MEMBERS, LANES))


def first_kernel(
    blocks, depth, chunk, parts, r_hbm, m_hbm, pair_ref, g_ref, r_ref, m_buf, acc_ref, r_sem, m_sem
):
    rows, n = m_hbm.shape
    block = rows // blocks

    def copy(i):
        slot = lax.rem(i, depth)
        at = pl.ds(pl.multiple_of(i * block, block), block)
        return pltpu.make_async_copy(m_hbm.at[at], m_buf.at[slot], m_sem.at[slot])

    vectors = pltpu.make_async_copy(r_hbm, r_ref, r_sem)
    copy(0).start()
    vectors.start()
    for i in range(1, depth):
        copy(i).start()
    acc_ref[...] = jnp.zeros_like(acc_ref)
    vectors.wait()

    def step(i, carry):
        copy(i).wait()
        slot = lax.rem(i, depth)
        for k in range(0, block, chunk):
            at = pl.ds(pl.multiple_of(i * block + k, chunk), chunk)
            pair = jnp.concatenate(split(m_buf[slot, k : k + chunk, :], 2), axis=1)
            pair_ref[at, :] = pair
            r = jnp.concatenate(split(r_ref[:, at], parts), axis=0)
            acc_ref[...] += jnp.dot(r, pair, preferred_element_type=F32)

        @pl.when(i + depth < blocks)
        def _():
            copy(i + depth).start()

        return carry

    lax.fori_loop(0, blocks, step, 0)
    g_ref[...] = fold(acc_ref[...], parts)


def first(residual, matrix, blocks=8, depth=3, chunk=512, parts=3):
    rows, n = matrix.shape
    return pl.pallas_call(
        functools.partial(first_kernel, blocks, depth, chunk, parts),
        in_specs=[ANY, ANY],
        out_specs=[VMEM, VMEM],
        out_shape=[pltpu.VMEM((rows, 2 * n), BF), pltpu.VMEM((MEMBERS, n), F32)],
        scratch_shapes=[
            pltpu.VMEM(residual.shape, F32),
            pltpu.VMEM((depth, rows // blocks, n), F32),
            pltpu.VMEM((MEMBERS * parts, 2 * n), F32),
            pltpu.SemaphoreType.DMA,
            pltpu.SemaphoreType.DMA((depth,)),
        ],
        compiler_params=params(16),
    )(far(residual), far(matrix))


def rows_body(slots, half, start, d, pair_ref, outs, w_ref, parts=3, chunk=512):
    rows, n2 = pair_ref.shape
    piece = rows // (2 * PIECES)
    vectors = jnp.concatenate([x.astype(F32) for x in split(d, parts)], axis=0)
    w_ref[: n2 // 2, :] = vectors.T.astype(BF)
    w_ref[n2 // 2 :, :] = w_ref[: n2 // 2, :]
    norm = jnp.sum(d * d, axis=1, keepdims=True)
    for slot, out in zip(slots, outs):
        q = lax.rem(start + slot, PIECES)
        for r in range(0, piece, chunk):
            at = pl.multiple_of((half * PIECES + q) * piece + r, chunk)
            o = jnp.dot(
                pair_ref[pl.ds(at, chunk), :], w_ref[...], preferred_element_type=F32
            ).T
            o = sum(o[MEMBERS * j : MEMBERS * (j + 1)] for j in range(parts))
            put(out, o, r // LANES)
        put_sums(out, norm)


AWAY = (1, 2, 3)


def each(ref):
    return [ref.at[i] for i in range(ref.shape[0])]


def send_first_kernel(order, a, b, c, d, pair_ref, out_ref, g_ref, w_ref):
    g = sum_of_ring(order, (a, b, c, d))
    g_ref[...] = g
    rows_body(range(PIECES), *place(1), g, pair_ref, each(out_ref), w_ref)


def send_second_kernel(
    order, a, b, c, d, g0_ref, gamma_ref, pair_ref, out_ref, g_ref, alpha_ref, w_ref
):
    w = sum_of_ring(order, (a, b, c, d))
    g0 = g0_ref[...]
    alpha = gamma_ref[:, :1] / sums_of(w)
    alpha_ref[...] = wide(alpha)
    g = g0 - alpha * strips(w, g0.shape[1])
    g_ref[...] = g
    rows_body(range(PIECES), *place(1), g, pair_ref, each(out_ref), w_ref)


def keep_kernel(d_ref, pair_ref, out_ref, w_ref):
    rows_body(AWAY, *place(0), d_ref[...], pair_ref, each(out_ref), w_ref)


def near_kernel(d_ref, after_ref, pair_ref, out_ref, w_ref):
    rows_body((0,), *place(0), d_ref[...], pair_ref, [out_ref], w_ref)


def by_rows(kernel, operands, pair, shapes):
    return pl.pallas_call(
        kernel,
        in_specs=[VMEM] * (len(operands) + 1),
        out_specs=[VMEM] * len(shapes),
        out_shape=[pltpu.VMEM(s, F32) for s in shapes],
        scratch_shapes=[pltpu.VMEM((pair.shape[1], 3 * MEMBERS), BF)],
        compiler_params=params(8),
    )(*map(pin, operands), pin(pair))


def cols_body(half, start, order, pieces, pair_ref, parts=3):
    piece = pieces[0].shape[1]
    acc = jnp.zeros((MEMBERS * parts, pair_ref.shape[1]), F32)
    norm = jnp.zeros((MEMBERS, 1), F32)
    for i, p in enumerate(pieces):
        q = lax.rem(start - order[i] + PIECES, PIECES)
        at = pl.multiple_of((half * PIECES + q) * piece, piece)
        vectors = jnp.concatenate(split(p, parts), axis=0)
        acc += jnp.dot(vectors, pair_ref[pl.ds(at, piece), :], preferred_element_type=F32)
        norm += jnp.sum(p * p, axis=1, keepdims=True)
    return fold(acc, parts), norm


def cols_own_kernel(order, a, b, c, d, pair_ref, w_ref):
    piece = pair_ref.shape[0] // (2 * PIECES)
    pieces = [strips(p, piece) for p in (a, b, c, d)]
    w, norm = cols_body(*place(0), order, pieces, pair_ref)
    put(w_ref, w)
    put_sums(w_ref, norm)


def cols_other_kernel(order, p_ref, before_ref, pair_ref, w_ref):
    piece = pair_ref.shape[0] // (2 * PIECES)
    pieces = [strips(p, piece) for p in each(p_ref)]
    w, norm = cols_body(*place(1), order, pieces, pair_ref)
    put(w_ref, w + strips(before_ref, w.shape[1]))
    put_sums(w_ref, norm + sums_of(before_ref))


def on_core(kernel, operands, shapes):
    return pl.pallas_call(
        kernel,
        in_specs=[VMEM] * len(operands),
        out_specs=[VMEM] * len(shapes),
        out_shape=[pltpu.VMEM(s, F32) for s in shapes],
        compiler_params=params(8),
    )(*map(pin, operands))


def ring(stage):
    def moved(f, k):
        z, x, core = f // 8, f // 2 % 4, f % 2
        if core == stage:
            z = (z + k) % 4
        else:
            x = (x + k) % 4
        return z * 8 + x * 2 + core

    return [[(f, moved(f, k)) for f in range(32)] for k in (1, 2, 3)]


CORE = [(f, f ^ 1) for f in range(32)]
CONF = [[(c, (c + k) % 4) for c in range(4)] for k in (1, 2, 3)]


def three(xs, axis, perms):
    return [lax.ppermute(x, axis, perm) for x, perm in zip(xs, perms)]


LAST, SECOND = (0, 1, 3, 2), (0, 2, 1, 3)


def listed(order, x):
    return [x[k] for k in order]


def sum_of_ring(order, refs):
    a, b, c, d = [refs[order.index(k)][...] for k in range(4)]
    return (a + c) + (b + d)


def total(own, others):
    return (others[0] + others[2]) + (own + others[1])


def reduce_pieces(order, d, send, pair):
    shape = send.shape[1:]
    got = lax.ppermute(send, "feat", CORE)
    (keep,) = by_rows(keep_kernel, [d], pair, [(len(AWAY), *shape)])
    away = [keep[i - 1] + got[i] for i in AWAY]
    (near,) = by_rows(near_kernel, [d, away[0]], pair, [shape])
    b, c, d = three(away, "feat", ring(0))
    piece = (d + b) + (c + (near + got[0]))
    return listed(order, [piece] + three([piece] * 3, "feat", ring(1)))


def piece_kernel(order, a, b, c, d, p_ref, gamma_ref):
    p = sum_of_ring(order, (a, b, c, d))
    p_ref[...] = p[: p_ref.shape[0]]
    gamma_ref[...] = wide(sums_of(p))


def image_kernel(order, a, b, c, d, before_ref, gamma0_ref, p_ref, gamma_ref):
    p = sum_of_ring(order, (a, b, c, d))
    gamma = sums_of(p)
    beta = gamma / gamma0_ref[:, :1]
    gamma_ref[...] = wide(gamma)
    for at in range(0, p_ref.shape[0], MEMBERS):
        p_ref[at : at + MEMBERS, :] = (
            p[at : at + MEMBERS] + beta * before_ref[at : at + MEMBERS, :]
        )


def curve_kernel(a, b, c, d, curve_ref):
    norm = sum(jnp.sum(strips(p, p.shape[0] * LANES // MEMBERS) ** 2, axis=1, keepdims=True) for p in (a, b, c, d))
    curve_ref[...] = wide(norm)


def gather_pieces(order, piece):
    own = listed(order, [piece] + three([piece] * 3, "feat", ring(0)))
    return own, jnp.stack(own)


def finish_kernel(p_order, i_order, *refs):
    r0_ref, alpha0_ref, gamma0_ref, gamma1_ref, curve_ref = refs[:5]
    p_own, p_other, i_own, i_other = refs[5:9], refs[9], refs[10:14], refs[14]
    g0_ref, g1_ref, sol_ref, res_ref = refs[15:]
    gamma1 = gamma1_ref[:, :1]
    a0 = alpha0_ref[:, :1]
    a1 = gamma1 / curve_ref[:, :1]
    b0 = gamma1 / gamma0_ref[:, :1]
    g0 = g0_ref[...]
    sol_ref[...] = a0 * g0 + a1 * (g1_ref[...] + b0 * g0)
    piece = p_own[0].shape[0] * LANES // MEMBERS
    for far_half, ps, images in ((0, p_own, i_own), (1, each(p_other), each(i_other))):
        half, start = place(far_half)
        for k in range(PIECES):
            q = lax.rem(start - k + PIECES, PIECES)
            at = pl.ds(pl.multiple_of((half * PIECES + q) * piece, piece), piece)
            p = strips(ps[p_order.index(k)], piece)
            image = strips(images[i_order.index(k)], piece)
            res_ref[:, at] = r0_ref[:, at] - a0 * p - a1 * image


ORDERS = (SECOND, SECOND, LAST, SECOND, SECOND, SECOND)


def body(matrix, targets):
    rows, n = matrix.shape
    size = rows // (2 * PIECES) * MEMBERS // LANES
    column = (MEMBERS, LANES)

    pair, part = first(targets, matrix)
    order = ORDERS[0]
    parts = listed(order, [part] + three([part] * 3, "conf", CONF))

    all_pieces = (PIECES, size + TAIL, LANES)
    send, g0 = by_rows(
        functools.partial(send_first_kernel, order), parts, pair, [all_pieces, (MEMBERS, n)])
    order = ORDERS[1]
    summands = reduce_pieces(order, g0, send, pair)
    p, gamma0 = on_core(
        functools.partial(piece_kernel, order), summands, [(size, LANES), column])
    p_own, stacked = gather_pieces(ORDERS[2], p)
    p_other = lax.ppermute(stacked, "feat", CORE)

    packed = [(MEMBERS * n // LANES + TAIL, LANES)]
    (w,) = on_core(functools.partial(cols_own_kernel, ORDERS[2]), p_own + [pair], packed)
    (w,) = on_core(functools.partial(cols_other_kernel, ORDERS[2]), [p_other, w, pair], packed)
    order = ORDERS[3]
    parts = listed(order, [w] + three([w] * 3, "conf", CONF))

    send, g1, alpha0 = by_rows(
        functools.partial(send_second_kernel, order), parts + [g0, gamma0], pair, [all_pieces, (MEMBERS, n), column]
    )
    order = ORDERS[4]
    summands = reduce_pieces(order, g1, send, pair)
    image, gamma1 = on_core(
        functools.partial(image_kernel, order), summands + [p, gamma0], [(size, LANES), column]
    )
    i_own, stacked = gather_pieces(ORDERS[5], image)

    (curve,) = on_core(curve_kernel, i_own, [column])
    curve = curve + lax.ppermute(curve, "feat", CORE)
    curve = total(curve, three([curve] * 3, "conf", CONF))
    i_other = lax.ppermute(stacked, "feat", CORE)

    return pl.pallas_call(
        functools.partial(finish_kernel, ORDERS[2], ORDERS[5]),
        in_specs=[VMEM] * 17,
        out_specs=[VMEM, VMEM],
        out_shape=[
            jax.ShapeDtypeStruct((MEMBERS, n), F32),
            jax.ShapeDtypeStruct((MEMBERS, rows), F32),
        ],
        compiler_params=params(8),
    )(
        targets,
        alpha0,
        gamma0,
        gamma1,
        curve,
        *p_own,
        p_other,
        *i_own,
        i_other,
        g0,
        g1,
    )


def solution(mesh):
    placed = (P("conf", "feat"), P(None, "conf"))
    return jax.shard_map(
        body,
        mesh=mesh,
        in_specs=placed,
        out_specs=(P(None, "feat"), P(None, "conf")),
        check_vma=False,
    )
```

```python
import functools

import jax
import jax.numpy as jnp
from jax import lax
from jax.experimental import pallas as pl
from jax.experimental.pallas import tpu as pltpu
from jax.sharding import PartitionSpec as P

BF, F32 = jnp.bfloat16, jnp.float32
MEMBERS = 32
PIECES = 4
LANES = 128
TAIL = 8
VMEM = pl.BlockSpec(memory_space=pltpu.VMEM)
ANY = pl.BlockSpec(memory_space=pl.ANY)


def params(mib):
    return pltpu.CompilerParams(vmem_limit_bytes=mib << 20)


def pin(x):
    return pltpu.with_memory_space_constraint(x, pltpu.VMEM)


def far(x):
    return pltpu.with_memory_space_constraint(x, pltpu.HBM)


def place(other):
    f = lax.axis_index("feat")
    z, x, core = f // 8, f // 2 % 4, f % 2
    return core ^ other, jnp.where((core ^ other) == 0, z, x)


def split(x, parts):
    out = []
    for _ in range(parts - 1):
        high = x.astype(BF)
        out.append(high)
        x = x - high.astype(F32)
    return out + [x.astype(BF)]


def fold(product, parts):
    n = product.shape[1] // 2
    rows = sum(product[MEMBERS * j : MEMBERS * (j + 1)] for j in range(parts))
    return rows[:, :n] + rows[:, n:]


def strips(packed_ref, width):
    at = range(0, width // LANES * MEMBERS, MEMBERS)
    return jnp.concatenate([packed_ref[i : i + MEMBERS, :] for i in at], axis=1)


def put(packed_ref, values, first=0):
    for j in range(values.shape[1] // LANES):
        at = (first + j) * MEMBERS
        packed_ref[at : at + MEMBERS, :] = values[:, j * LANES : (j + 1) * LANES]


def put_sums(packed_ref, column):
    groups = MEMBERS // TAIL
    blocks = [column[TAIL * k : TAIL * (k + 1)] for k in range(groups)]
    blocks = [jnp.broadcast_to(b, (TAIL, LANES // groups)) for b in blocks]
    packed_ref[packed_ref.shape[0] - TAIL :, :] = jnp.concatenate(blocks, axis=1)


def sums_of(packed):
    groups = MEMBERS // TAIL
    block, width = packed[packed.shape[0] - TAIL :, :], LANES // groups
    return jnp.concatenate(
        [block[:, k * width : k * width + 1] for k in range(groups)], axis=0
    )


def wide(column):
    return jnp.broadcast_to(column, (MEMBERS, LANES))


def first_kernel(
    blocks, depth, chunk, parts, r_hbm, m_hbm, pair_ref, g_ref, r_ref, m_buf, acc_ref, r_sem, m_sem
):
    rows, n = m_hbm.shape
    block = rows // blocks

    def copy(i):
        slot = lax.rem(i, depth)
        at = pl.ds(pl.multiple_of(i * block, block), block)
        return pltpu.make_async_copy(m_hbm.at[at], m_buf.at[slot], m_sem.at[slot])

    vectors = pltpu.make_async_copy(r_hbm, r_ref, r_sem)
    copy(0).start()
    vectors.start()
    for i in range(1, depth):
        copy(i).start()
    acc_ref[...] = jnp.zeros_like(acc_ref)
    vectors.wait()

    def step(i, carry):
        copy(i).wait()
        slot = lax.rem(i, depth)
        for k in range(0, block, chunk):
            at = pl.ds(pl.multiple_of(i * block + k, chunk), chunk)
            pair = jnp.concatenate(split(m_buf[slot, k : k + chunk, :], 2), axis=1)
            pair_ref[at, :] = pair
            r = jnp.concatenate(split(r_ref[:, at], parts), axis=0)
            acc_ref[...] += jnp.dot(r, pair, preferred_element_type=F32)

        @pl.when(i + depth < blocks)
        def _():
            copy(i + depth).start()

        return carry

    lax.fori_loop(0, blocks, step, 0)
    g_ref[...] = fold(acc_ref[...], parts)


def first(residual, matrix, blocks=8, depth=3, chunk=512, parts=3):
    rows, n = matrix.shape
    return pl.pallas_call(
        functools.partial(first_kernel, blocks, depth, chunk, parts),
        in_specs=[ANY, ANY],
        out_specs=[VMEM, VMEM],
        out_shape=[pltpu.VMEM((rows, 2 * n), BF), pltpu.VMEM((MEMBERS, n), F32)],
        scratch_shapes=[
            pltpu.VMEM(residual.shape, F32),
            pltpu.VMEM((depth, rows // blocks, n), F32),
            pltpu.VMEM((MEMBERS * parts, 2 * n), F32),
            pltpu.SemaphoreType.DMA,
            pltpu.SemaphoreType.DMA((depth,)),
        ],
        compiler_params=params(11),
    )(far(residual), far(matrix))


def rows_body(slots, half, start, d, pair_ref, outs, w_ref, parts=3, chunk=512):
    rows, n2 = pair_ref.shape
    piece = rows // (2 * PIECES)
    vectors = jnp.concatenate([x.astype(F32) for x in split(d, parts)], axis=0)
    w_ref[: n2 // 2, :] = vectors.T.astype(BF)
    w_ref[n2 // 2 :, :] = w_ref[: n2 // 2, :]
    norm = jnp.sum(d * d, axis=1, keepdims=True)
    for slot, out in zip(slots, outs):
        q = start ^ slot
        for r in range(0, piece, chunk):
            at = pl.multiple_of((half * PIECES + q) * piece + r, chunk)
            o = jnp.dot(
                pair_ref[pl.ds(at, chunk), :], w_ref[...], preferred_element_type=F32
            ).T
            o = sum(o[MEMBERS * j : MEMBERS * (j + 1)] for j in range(parts))
            put(out, o, r // LANES)
        put_sums(out, norm)


AWAY = (1, 2, 3)
FLIP = (1, 2, 3)


def flip_kernel(chunk, pair_ref, flipped_ref):
    piece = flipped_ref.shape[1] // len(FLIP)
    half, start = place(1)
    for i, slot in enumerate(FLIP):
        q = start ^ slot
        for r in range(0, piece, chunk):
            at = pl.multiple_of((half * PIECES + q) * piece + r, chunk)
            to = i * piece + r
            flipped_ref[:, to : to + chunk] = pair_ref[pl.ds(at, chunk), :].T


def flip(pair, chunk=512):
    rows, n2 = pair.shape
    return pl.pallas_call(
        functools.partial(flip_kernel, chunk),
        in_specs=[VMEM],
        out_specs=VMEM,
        out_shape=pltpu.VMEM((n2, rows // (2 * PIECES) * len(FLIP)), BF),
        compiler_params=params(4),
        cost_estimate=pl.CostEstimate(
            flops=0, bytes_accessed=2 * rows * n2, transcendentals=0
        ),
    )(pin(pair))


def rows_flipped(d, flipped_ref, outs, parts=3, chunk=512):
    piece = flipped_ref.shape[1] // len(FLIP)
    vectors = jnp.concatenate(split(d, parts), axis=0)
    vectors = jnp.concatenate([vectors, vectors], axis=1)
    norm = jnp.sum(d * d, axis=1, keepdims=True)
    for i, out in enumerate(outs):
        for r in range(0, piece, chunk):
            at = i * piece + r
            o = jnp.dot(
                vectors, flipped_ref[:, at : at + chunk], preferred_element_type=F32
            )
            o = sum(o[MEMBERS * j : MEMBERS * (j + 1)] for j in range(parts))
            put(out, o, r // LANES)
        put_sums(out, norm)


def each(ref):
    return [ref.at[i] for i in range(ref.shape[0])]


def send_first_kernel(order, a, b, c, d, flipped_ref, pair_ref, out_ref, g_ref, w_ref):
    g = sum_of_ring(order, (a, b, c, d))
    g_ref[...] = g
    rest = [k for k in range(PIECES) if k not in FLIP]
    rows_flipped(g, flipped_ref, [out_ref.at[k] for k in FLIP])
    rows_body(rest, *place(1), g, pair_ref, [out_ref.at[k] for k in rest], w_ref)


def send_second_kernel(
    order, a, b, c, d, g0_ref, gamma_ref, flipped_ref, pair_ref, out_ref, g_ref, alpha_ref, w_ref
):
    w = sum_of_ring(order, (a, b, c, d))
    g0 = g0_ref[...]
    alpha = gamma_ref[:, :1] / sums_of(w)
    alpha_ref[...] = wide(alpha)
    g = g0 - alpha * strips(w, g0.shape[1])
    g_ref[...] = g
    rest = [k for k in range(PIECES) if k not in FLIP]
    rows_flipped(g, flipped_ref, [out_ref.at[k] for k in FLIP])
    rows_body(rest, *place(1), g, pair_ref, [out_ref.at[k] for k in rest], w_ref)


def keep_kernel(d_ref, pair_ref, out_ref, w_ref):
    rows_body(AWAY, *place(0), d_ref[...], pair_ref, each(out_ref), w_ref)


def near_kernel(d_ref, after_ref, pair_ref, out_ref, w_ref):
    rows_body((0,), *place(0), d_ref[...], pair_ref, [out_ref], w_ref)


def by_rows(kernel, operands, pair, shapes):
    return pl.pallas_call(
        kernel,
        in_specs=[VMEM] * (len(operands) + 1),
        out_specs=[VMEM] * len(shapes),
        out_shape=[pltpu.VMEM(s, F32) for s in shapes],
        scratch_shapes=[pltpu.VMEM((pair.shape[1], 3 * MEMBERS), BF)],
        compiler_params=params(4),
    )(*map(pin, operands), pin(pair))


def cols_body(half, start, order, pieces, pair_ref, parts=3):
    piece = pieces[0].shape[1]
    acc = jnp.zeros((MEMBERS * parts, pair_ref.shape[1]), F32)
    norm = jnp.zeros((MEMBERS, 1), F32)
    for i, p in enumerate(pieces):
        q = start ^ order[i]
        at = pl.multiple_of((half * PIECES + q) * piece, piece)
        vectors = jnp.concatenate(split(p, parts), axis=0)
        acc += jnp.dot(vectors, pair_ref[pl.ds(at, piece), :], preferred_element_type=F32)
        norm += jnp.sum(p * p, axis=1, keepdims=True)
    return fold(acc, parts), norm


def cols_own_kernel(order, a, b, c, d, pair_ref, w_ref):
    piece = pair_ref.shape[0] // (2 * PIECES)
    pieces = [strips(p, piece) for p in (a, b, c, d)]
    w, norm = cols_body(*place(0), order, pieces, pair_ref)
    put(w_ref, w)
    put_sums(w_ref, norm)


def cols_other_kernel(order, p_ref, before_ref, pair_ref, w_ref):
    piece = pair_ref.shape[0] // (2 * PIECES)
    pieces = [strips(p, piece) for p in each(p_ref)]
    w, norm = cols_body(*place(1), order, pieces, pair_ref)
    put(w_ref, w + strips(before_ref, w.shape[1]))
    put_sums(w_ref, norm + sums_of(before_ref))


def on_core(kernel, operands, shapes):
    return pl.pallas_call(
        kernel,
        in_specs=[VMEM] * len(operands),
        out_specs=[VMEM] * len(shapes),
        out_shape=[pltpu.VMEM(s, F32) for s in shapes],
        compiler_params=params(4),
    )(*map(pin, operands))


def ring(stage):
    def moved(f, k):
        z, x, core = f // 8, f // 2 % 4, f % 2
        if core == stage:
            z = z ^ k
        else:
            x = x ^ k
        return z * 8 + x * 2 + core

    return [[(f, moved(f, k)) for f in range(32)] for k in (1, 2, 3)]


CORE = [(f, f ^ 1) for f in range(32)]
CONF = [[(c, c ^ k) for c in range(4)] for k in (1, 2, 3)]


def three(xs, axis, perms):
    return [lax.ppermute(x, axis, perm) for x, perm in zip(xs, perms)]


LAST, SECOND = (0, 1, 3, 2), (0, 2, 1, 3)


def listed(order, x):
    return [x[k] for k in order]


def sum_of_ring(order, refs):
    a, b, c, d = [refs[order.index(k)][...] for k in range(4)]
    return (a + c) + (b + d)


def total(own, others):
    return (others[0] + others[2]) + (own + others[1])


def reduce_pieces(order, d, send, pair):
    shape = send.shape[1:]
    got = lax.ppermute(send, "feat", CORE)
    (keep,) = by_rows(keep_kernel, [d], pair, [(len(AWAY), *shape)])
    away = [keep[i - 1] + got[i] for i in AWAY]
    (near,) = by_rows(near_kernel, [d, away[0]], pair, [shape])
    b, c, d = three(away, "feat", ring(0))
    piece = (b + c) + (d + (near + got[0]))
    return listed(order, [piece] + three([piece] * 3, "feat", ring(1)))


def piece_kernel(order, a, b, c, d, p_ref, gamma_ref):
    p = sum_of_ring(order, (a, b, c, d))
    p_ref[...] = p[: p_ref.shape[0]]
    gamma_ref[...] = wide(sums_of(p))


def image_kernel(order, a, b, c, d, before_ref, gamma0_ref, p_ref, gamma_ref):
    p = sum_of_ring(order, (a, b, c, d))
    gamma = sums_of(p)
    beta = gamma / gamma0_ref[:, :1]
    gamma_ref[...] = wide(gamma)
    for at in range(0, p_ref.shape[0], MEMBERS):
        p_ref[at : at + MEMBERS, :] = (
            p[at : at + MEMBERS] + beta * before_ref[at : at + MEMBERS, :]
        )


def curve_kernel(a, b, c, d, curve_ref):
    norm = sum(jnp.sum(strips(p, p.shape[0] * LANES // MEMBERS) ** 2, axis=1, keepdims=True) for p in (a, b, c, d))
    curve_ref[...] = wide(norm)


def gather_pieces(order, piece):
    own = listed(order, [piece] + three([piece] * 3, "feat", ring(0)))
    return own, jnp.stack(own)


def finish_kernel(p_order, i_order, *refs):
    r0_ref, alpha0_ref, gamma0_ref, gamma1_ref, curve_ref = refs[:5]
    p_own, p_other, i_own, i_other = refs[5:9], refs[9], refs[10:14], refs[14]
    g0_ref, g1_ref, sol_ref, res_ref = refs[15:]
    gamma1 = gamma1_ref[:, :1]
    a0 = alpha0_ref[:, :1]
    a1 = gamma1 / curve_ref[:, :1]
    b0 = gamma1 / gamma0_ref[:, :1]
    g0 = g0_ref[...]
    sol_ref[...] = a0 * g0 + a1 * (g1_ref[...] + b0 * g0)
    piece = p_own[0].shape[0] * LANES // MEMBERS
    for far_half, ps, images in ((0, p_own, i_own), (1, each(p_other), each(i_other))):
        half, start = place(far_half)
        for k in range(PIECES):
            q = start ^ k
            at = pl.ds(pl.multiple_of((half * PIECES + q) * piece, piece), piece)
            p = strips(ps[p_order.index(k)], piece)
            image = strips(images[i_order.index(k)], piece)
            res_ref[:, at] = r0_ref[:, at] - a0 * p - a1 * image


ORDERS = (LAST, LAST, LAST, LAST, LAST, LAST)


def body(matrix, targets):
    rows, n = matrix.shape
    size = rows // (2 * PIECES) * MEMBERS // LANES
    column = (MEMBERS, LANES)

    pair, part = first(targets, matrix)
    flipped = flip(pair)
    order = ORDERS[0]
    parts = listed(order, [part] + three([part] * 3, "conf", CONF))

    all_pieces = (PIECES, size + TAIL, LANES)
    send, g0 = by_rows(
        functools.partial(send_first_kernel, order), parts + [flipped], pair, [all_pieces, (MEMBERS, n)])
    order = ORDERS[1]
    summands = reduce_pieces(order, g0, send, pair)
    p, gamma0 = on_core(
        functools.partial(piece_kernel, order), summands, [(size, LANES), column])
    p_own, stacked = gather_pieces(ORDERS[2], p)
    p_other = lax.ppermute(stacked, "feat", CORE)

    packed = [(MEMBERS * n // LANES + TAIL, LANES)]
    (w,) = on_core(functools.partial(cols_own_kernel, ORDERS[2]), p_own + [pair], packed)
    (w,) = on_core(functools.partial(cols_other_kernel, ORDERS[2]), [p_other, w, pair], packed)
    order = ORDERS[3]
    parts = listed(order, [w] + three([w] * 3, "conf", CONF))

    send, g1, alpha0 = by_rows(
        functools.partial(send_second_kernel, order), parts + [g0, gamma0, flipped], pair, [all_pieces, (MEMBERS, n), column]
    )
    order = ORDERS[4]
    summands = reduce_pieces(order, g1, send, pair)
    image, gamma1 = on_core(
        functools.partial(image_kernel, order), summands + [p, gamma0], [(size, LANES), column]
    )
    i_own, stacked = gather_pieces(ORDERS[5], image)

    (curve,) = on_core(curve_kernel, i_own, [column])
    curve = curve + lax.ppermute(curve, "feat", CORE)
    curve = total(curve, three([curve] * 3, "conf", CONF))
    i_other = lax.ppermute(stacked, "feat", CORE)

    return pl.pallas_call(
        functools.partial(finish_kernel, ORDERS[2], ORDERS[5]),
        in_specs=[VMEM] * 17,
        out_specs=[VMEM, VMEM],
        out_shape=[
            jax.ShapeDtypeStruct((MEMBERS, n), F32),
            jax.ShapeDtypeStruct((MEMBERS, rows), F32),
        ],
        compiler_params=params(4),
    )(
        targets,
        alpha0,
        gamma0,
        gamma1,
        curve,
        *p_own,
        p_other,
        *i_own,
        i_other,
        g0,
        g1,
    )


def solution(mesh):
    placed = (P("conf", "feat"), P(None, "conf"))
    return jax.shard_map(
        body,
        mesh=mesh,
        in_specs=placed,
        out_specs=(P(None, "feat"), P(None, "conf")),
        check_vma=False,
    )
```

```python
import functools

import jax
import jax.numpy as jnp
from jax import lax
from jax.experimental import pallas as pl
from jax.experimental.pallas import tpu as pltpu
from jax.sharding import PartitionSpec as P

BF, F32 = jnp.bfloat16, jnp.float32
MEMBERS = 32
PIECES = 4
LANES = 128
TAIL = 8
VMEM = pl.BlockSpec(memory_space=pltpu.VMEM)
ANY = pl.BlockSpec(memory_space=pl.ANY)


def params(mib):
    return pltpu.CompilerParams(vmem_limit_bytes=mib << 20)


def pin(x):
    return pltpu.with_memory_space_constraint(x, pltpu.VMEM)


def far(x):
    return pltpu.with_memory_space_constraint(x, pltpu.HBM)


def place(other):
    f = lax.axis_index("feat")
    z, x, core = f // 8, f // 2 % 4, f % 2
    return core ^ other, jnp.where((core ^ other) == 0, z, x)


def split(x, parts):
    out = []
    for _ in range(parts - 1):
        high = x.astype(BF)
        out.append(high)
        x = x - high.astype(F32)
    return out + [x.astype(BF)]


def fold(product, parts):
    n = product.shape[1] // 2
    rows = sum(product[MEMBERS * j : MEMBERS * (j + 1)] for j in range(parts))
    return rows[:, :n] + rows[:, n:]


def strips(packed_ref, width):
    at = range(0, width // LANES * MEMBERS, MEMBERS)
    return jnp.concatenate([packed_ref[i : i + MEMBERS, :] for i in at], axis=1)


def put(packed_ref, values, first=0):
    for j in range(values.shape[1] // LANES):
        at = (first + j) * MEMBERS
        packed_ref[at : at + MEMBERS, :] = values[:, j * LANES : (j + 1) * LANES]


def put_sums(packed_ref, column):
    groups = MEMBERS // TAIL
    blocks = [column[TAIL * k : TAIL * (k + 1)] for k in range(groups)]
    blocks = [jnp.broadcast_to(b, (TAIL, LANES // groups)) for b in blocks]
    packed_ref[packed_ref.shape[0] - TAIL :, :] = jnp.concatenate(blocks, axis=1)


def sums_of(packed):
    groups = MEMBERS // TAIL
    block, width = packed[packed.shape[0] - TAIL :, :], LANES // groups
    return jnp.concatenate(
        [block[:, k * width : k * width + 1] for k in range(groups)], axis=0
    )


def wide(column):
    return jnp.broadcast_to(column, (MEMBERS, LANES))


def first_kernel(
    blocks, depth, chunk, parts, r_hbm, m_hbm, pair_ref, g_ref, r_ref, m_buf, acc_ref, r_sem, m_sem
):
    rows, n = m_hbm.shape
    block = rows // blocks

    def copy(i):
        slot = lax.rem(i, depth)
        at = pl.ds(pl.multiple_of(i * block, block), block)
        return pltpu.make_async_copy(m_hbm.at[at], m_buf.at[slot], m_sem.at[slot])

    vectors = pltpu.make_async_copy(r_hbm, r_ref, r_sem)
    copy(0).start()
    vectors.start()
    for i in range(1, depth):
        copy(i).start()
    acc_ref[...] = jnp.zeros_like(acc_ref)
    vectors.wait()

    def step(i, carry):
        copy(i).wait()
        slot = lax.rem(i, depth)
        for k in range(0, block, chunk):
            at = pl.ds(pl.multiple_of(i * block + k, chunk), chunk)
            pair = jnp.concatenate(split(m_buf[slot, k : k + chunk, :], 2), axis=1)
            pair_ref[at, :] = pair
            r = jnp.concatenate(split(r_ref[:, at], parts), axis=0)
            acc_ref[...] += jnp.dot(r, pair, preferred_element_type=F32)

        @pl.when(i + depth < blocks)
        def _():
            copy(i + depth).start()

        return carry

    lax.fori_loop(0, blocks, step, 0)
    g_ref[...] = fold(acc_ref[...], parts)


def first(residual, matrix, blocks=8, depth=4, chunk=512, parts=3):
    rows, n = matrix.shape
    return pl.pallas_call(
        functools.partial(first_kernel, blocks, depth, chunk, parts),
        in_specs=[ANY, ANY],
        out_specs=[VMEM, VMEM],
        out_shape=[pltpu.VMEM((rows, 2 * n), BF), pltpu.VMEM((MEMBERS, n), F32)],
        scratch_shapes=[
            pltpu.VMEM(residual.shape, F32),
            pltpu.VMEM((depth, rows // blocks, n), F32),
            pltpu.VMEM((MEMBERS * parts, 2 * n), F32),
            pltpu.SemaphoreType.DMA,
            pltpu.SemaphoreType.DMA((depth,)),
        ],
        compiler_params=params(14),
    )(far(residual), far(matrix))


def rows_body(slots, half, start, d, pair_ref, outs, w_ref, parts=3, chunk=512):
    rows, n2 = pair_ref.shape
    piece = rows // (2 * PIECES)
    vectors = jnp.concatenate([x.astype(F32) for x in split(d, parts)], axis=0)
    w_ref[: n2 // 2, :] = vectors.T.astype(BF)
    w_ref[n2 // 2 :, :] = w_ref[: n2 // 2, :]
    norm = jnp.sum(d * d, axis=1, keepdims=True)
    for slot, out in zip(slots, outs):
        q = start ^ slot
        for r in range(0, piece, chunk):
            at = pl.multiple_of((half * PIECES + q) * piece + r, chunk)
            o = jnp.dot(
                pair_ref[pl.ds(at, chunk), :], w_ref[...], preferred_element_type=F32
            ).T
            o = sum(o[MEMBERS * j : MEMBERS * (j + 1)] for j in range(parts))
            put(out, o, r // LANES)
        put_sums(out, norm)


AWAY = (1, 2, 3)
FLIP = (1, 2, 3)


def flip_kernel(chunk, pair_ref, flipped_ref):
    piece = flipped_ref.shape[1] // len(FLIP)
    half, start = place(1)
    for i, slot in enumerate(FLIP):
        q = start ^ slot
        for r in range(0, piece, chunk):
            at = pl.multiple_of((half * PIECES + q) * piece + r, chunk)
            to = i * piece + r
            flipped_ref[:, to : to + chunk] = pair_ref[pl.ds(at, chunk), :].T


def flip(pair, chunk=512):
    rows, n2 = pair.shape
    return pl.pallas_call(
        functools.partial(flip_kernel, chunk),
        in_specs=[VMEM],
        out_specs=VMEM,
        out_shape=pltpu.VMEM((n2, rows // (2 * PIECES) * len(FLIP)), BF),
        compiler_params=params(4),
        cost_estimate=pl.CostEstimate(
            flops=0, bytes_accessed=2 * rows * n2, transcendentals=0
        ),
    )(pin(pair))


def rows_flipped(d, flipped_ref, outs, parts=3, chunk=512):
    piece = flipped_ref.shape[1] // len(FLIP)
    vectors = jnp.concatenate(split(d, parts), axis=0)
    vectors = jnp.concatenate([vectors, vectors], axis=1)
    norm = jnp.sum(d * d, axis=1, keepdims=True)
    for i, out in enumerate(outs):
        for r in range(0, piece, chunk):
            at = i * piece + r
            o = jnp.dot(
                vectors, flipped_ref[:, at : at + chunk], preferred_element_type=F32
            )
            o = sum(o[MEMBERS * j : MEMBERS * (j + 1)] for j in range(parts))
            put(out, o, r // LANES)
        put_sums(out, norm)


def each(ref):
    return [ref.at[i] for i in range(ref.shape[0])]


def send_first_kernel(order, a, b, c, d, flipped_ref, pair_ref, out_ref, g_ref, w_ref):
    g = sum_of_ring(order, (a, b, c, d))
    g_ref[...] = g
    rest = [k for k in range(PIECES) if k not in FLIP]
    rows_flipped(g, flipped_ref, [out_ref.at[k] for k in FLIP])
    rows_body(rest, *place(1), g, pair_ref, [out_ref.at[k] for k in rest], w_ref)


def send_second_kernel(
    order, a, b, c, d, g0_ref, gamma_ref, flipped_ref, pair_ref, out_ref, g_ref, alpha_ref, w_ref
):
    w = sum_of_ring(order, (a, b, c, d))
    g0 = g0_ref[...]
    alpha = gamma_ref[:, :1] / sums_of(w)
    alpha_ref[...] = wide(alpha)
    g = g0 - alpha * strips(w, g0.shape[1])
    g_ref[...] = g
    rest = [k for k in range(PIECES) if k not in FLIP]
    rows_flipped(g, flipped_ref, [out_ref.at[k] for k in FLIP])
    rows_body(rest, *place(1), g, pair_ref, [out_ref.at[k] for k in rest], w_ref)


def keep_kernel(d_ref, pair_ref, out_ref, w_ref):
    rows_body(AWAY, *place(0), d_ref[...], pair_ref, each(out_ref), w_ref)


def near_kernel(d_ref, after_ref, pair_ref, out_ref, w_ref):
    rows_body((0,), *place(0), d_ref[...], pair_ref, [out_ref], w_ref)


def by_rows(kernel, operands, pair, shapes):
    return pl.pallas_call(
        kernel,
        in_specs=[VMEM] * (len(operands) + 1),
        out_specs=[VMEM] * len(shapes),
        out_shape=[pltpu.VMEM(s, F32) for s in shapes],
        scratch_shapes=[pltpu.VMEM((pair.shape[1], 3 * MEMBERS), BF)],
        compiler_params=params(4),
    )(*map(pin, operands), pin(pair))


def cols_body(half, start, order, pieces, pair_ref, parts=3):
    piece = pieces[0].shape[1]
    acc = jnp.zeros((MEMBERS * parts, pair_ref.shape[1]), F32)
    norm = jnp.zeros((MEMBERS, 1), F32)
    for i, p in enumerate(pieces):
        q = start ^ order[i]
        at = pl.multiple_of((half * PIECES + q) * piece, piece)
        vectors = jnp.concatenate(split(p, parts), axis=0)
        acc += jnp.dot(vectors, pair_ref[pl.ds(at, piece), :], preferred_element_type=F32)
        norm += jnp.sum(p * p, axis=1, keepdims=True)
    return fold(acc, parts), norm


def cols_near_kernel(p_ref, pair_ref, w_ref):
    piece = pair_ref.shape[0] // (2 * PIECES)
    w, norm = cols_body(*place(0), (0,), [strips(p_ref, piece)], pair_ref)
    put(w_ref, w)
    put_sums(w_ref, norm)


def cols_own_kernel(order, b, c, d, before_ref, pair_ref, w_ref):
    piece = pair_ref.shape[0] // (2 * PIECES)
    pieces = [strips(p, piece) for p in (b, c, d)]
    w, norm = cols_body(*place(0), order[1:], pieces, pair_ref)
    put(w_ref, w + strips(before_ref, w.shape[1]))
    put_sums(w_ref, norm + sums_of(before_ref))


def cols_other_kernel(order, p_ref, before_ref, pair_ref, w_ref):
    piece = pair_ref.shape[0] // (2 * PIECES)
    pieces = [strips(p, piece) for p in each(p_ref)]
    w, norm = cols_body(*place(1), order, pieces, pair_ref)
    put(w_ref, w + strips(before_ref, w.shape[1]))
    put_sums(w_ref, norm + sums_of(before_ref))


def on_core(kernel, operands, shapes):
    return pl.pallas_call(
        kernel,
        in_specs=[VMEM] * len(operands),
        out_specs=[VMEM] * len(shapes),
        out_shape=[pltpu.VMEM(s, F32) for s in shapes],
        compiler_params=params(4),
    )(*map(pin, operands))


def ring(stage):
    def moved(f, k):
        z, x, core = f // 8, f // 2 % 4, f % 2
        if core == stage:
            z = z ^ k
        else:
            x = x ^ k
        return z * 8 + x * 2 + core

    return [[(f, moved(f, k)) for f in range(32)] for k in (1, 2, 3)]


CORE = [(f, f ^ 1) for f in range(32)]
CONF = [[(c, c ^ k) for c in range(4)] for k in (1, 2, 3)]


def three(xs, axis, perms):
    return [lax.ppermute(x, axis, perm) for x, perm in zip(xs, perms)]


LAST, SECOND = (0, 1, 3, 2), (0, 2, 1, 3)


def listed(order, x):
    return [x[k] for k in order]


def sum_of_ring(order, refs):
    a, b, c, d = [refs[order.index(k)][...] for k in range(4)]
    return (a + c) + (b + d)


def total(own, others):
    return (others[0] + others[2]) + (own + others[1])


def reduce_pieces(order, d, send, pair):
    shape = send.shape[1:]
    got = lax.ppermute(send, "feat", CORE)
    (keep,) = by_rows(keep_kernel, [d], pair, [(len(AWAY), *shape)])
    away = [keep[i - 1] + got[i] for i in AWAY]
    (near,) = by_rows(near_kernel, [d, away[0]], pair, [shape])
    b, c, d = three(away, "feat", ring(0))
    piece = (b + c) + (d + (near + got[0]))
    return listed(order, [piece] + three([piece] * 3, "feat", ring(1)))


def piece_kernel(order, a, b, c, d, p_ref, gamma_ref):
    p = sum_of_ring(order, (a, b, c, d))
    p_ref[...] = p[: p_ref.shape[0]]
    gamma_ref[...] = wide(sums_of(p))


def image_kernel(order, a, b, c, d, before_ref, gamma0_ref, p_ref, gamma_ref):
    p = sum_of_ring(order, (a, b, c, d))
    gamma = sums_of(p)
    beta = gamma / gamma0_ref[:, :1]
    gamma_ref[...] = wide(gamma)
    for at in range(0, p_ref.shape[0], MEMBERS):
        p_ref[at : at + MEMBERS, :] = (
            p[at : at + MEMBERS] + beta * before_ref[at : at + MEMBERS, :]
        )


def curve_kernel(a, b, c, d, curve_ref):
    width = a.shape[0] * LANES // MEMBERS
    squares = [jnp.square(strips(p, width)) for p in (a, b, c, d)]
    put_sums(curve_ref, jnp.sum(sum(squares), axis=1, keepdims=True))


def stack_kernel(a, b, c, d, after_ref, out_ref):
    for i, x in enumerate((a, b, c, d)):
        out_ref[i] = x[...]


def gather_pieces(order, piece, after):
    own = listed(order, [piece] + three([piece] * 3, "feat", ring(0)))
    (stacked,) = on_core(stack_kernel, own + [after], [(PIECES, *piece.shape)])
    return own, stacked


def finish_kernel(p_order, i_order, *refs):
    r0_ref, alpha0_ref, gamma0_ref, gamma1_ref, curve_ref = refs[:5]
    p_own, p_other, i_own, i_other = refs[5:9], refs[9], refs[10:14], refs[14]
    g0_ref, g1_ref, sol_ref, res_ref = refs[15:]
    gamma1 = gamma1_ref[:, :1]
    a0 = alpha0_ref[:, :1]
    a1 = gamma1 / sums_of(curve_ref[...])
    b0 = gamma1 / gamma0_ref[:, :1]
    g0 = g0_ref[...]
    sol_ref[...] = a0 * g0 + a1 * (g1_ref[...] + b0 * g0)
    piece = p_own[0].shape[0] * LANES // MEMBERS
    for far_half, ps, images in ((0, p_own, i_own), (1, each(p_other), each(i_other))):
        half, start = place(far_half)
        for k in range(PIECES):
            q = start ^ k
            at = pl.ds(pl.multiple_of((half * PIECES + q) * piece, piece), piece)
            p = strips(ps[p_order.index(k)], piece)
            image = strips(images[i_order.index(k)], piece)
            res_ref[:, at] = r0_ref[:, at] - a0 * p - a1 * image


ORDERS = (LAST, LAST, LAST, LAST, LAST, LAST)


def body(matrix, targets):
    rows, n = matrix.shape
    size = rows // (2 * PIECES) * MEMBERS // LANES
    column = (MEMBERS, LANES)

    pair, part = first(targets, matrix)
    flipped = flip(pair)
    order = ORDERS[0]
    parts = listed(order, [part] + three([part] * 3, "conf", CONF))

    all_pieces = (PIECES, size + TAIL, LANES)
    send, g0 = by_rows(
        functools.partial(send_first_kernel, order), parts + [flipped], pair, [all_pieces, (MEMBERS, n)])
    order = ORDERS[1]
    summands = reduce_pieces(order, g0, send, pair)
    p, gamma0 = on_core(
        functools.partial(piece_kernel, order), summands, [(size, LANES), column])
    packed = [(MEMBERS * n // LANES + TAIL, LANES)]
    (w,) = on_core(cols_near_kernel, [p, pair], packed)
    p_own, stacked = gather_pieces(ORDERS[2], p, w)
    p_other = lax.ppermute(stacked, "feat", CORE)

    (w,) = on_core(functools.partial(cols_own_kernel, ORDERS[2]), p_own[1:] + [w, pair], packed)
    (w,) = on_core(functools.partial(cols_other_kernel, ORDERS[2]), [p_other, w, pair], packed)
    order = ORDERS[3]
    parts = listed(order, [w] + three([w] * 3, "conf", CONF))

    send, g1, alpha0 = by_rows(
        functools.partial(send_second_kernel, order), parts + [g0, gamma0, flipped], pair, [all_pieces, (MEMBERS, n), column]
    )
    order = ORDERS[4]
    summands = reduce_pieces(order, g1, send, pair)
    image, gamma1 = on_core(
        functools.partial(image_kernel, order), summands + [p, gamma0], [(size, LANES), column]
    )
    i_own, stacked = gather_pieces(ORDERS[5], image, gamma1)

    (curve,) = on_core(curve_kernel, i_own, [(TAIL, LANES)])
    curve = curve + lax.ppermute(curve, "feat", CORE)
    curve = total(curve, three([curve] * 3, "conf", CONF))
    i_other = lax.ppermute(stacked, "feat", CORE)

    return pl.pallas_call(
        functools.partial(finish_kernel, ORDERS[2], ORDERS[5]),
        in_specs=[VMEM] * 17,
        out_specs=[VMEM, VMEM],
        out_shape=[
            jax.ShapeDtypeStruct((MEMBERS, n), F32),
            jax.ShapeDtypeStruct((MEMBERS, rows), F32),
        ],
        compiler_params=params(4),
    )(
        targets,
        alpha0,
        gamma0,
        gamma1,
        curve,
        *p_own,
        p_other,
        *i_own,
        i_other,
        g0,
        g1,
    )


def solution(mesh):
    placed = (P("conf", "feat"), P(None, "conf"))
    return jax.shard_map(
        body,
        mesh=mesh,
        in_specs=placed,
        out_specs=(P(None, "feat"), P(None, "conf")),
        check_vma=False,
    )
```
